32 devices in a mesh: groups: 2 (over x), dom: 8 (over z, y), slab: 2 (over core).
Axes of the slice: x: 2, y: 2, z: 4, core: 2. Of those that a mesh axis runs over, the one named last changes fastest.
Arguments:
- particles: float32 [16, 64, 128, 128], P(('groups', 'dom'), 'slab'), parts along dimension 0, may hold values from -3 to 3
- state_zero: bfloat16 [16, 64, 128, 128], P(('groups', 'dom'), 'slab'), parts along dimension 0, may hold values from -6 to 6
- state_one: bfloat16 [16, 64, 128, 128], P(('groups', 'dom'), 'slab'), parts along dimension 0, may hold values from -6 to 6
- source: float32 [128, 128, 128], P(('groups', 'slab')), parts along dimension 0, may hold values from -6 to 6
- observed: float32 [128, 128, 128], P(('groups', 'slab')), parts along dimension 0, may hold values from -6 to 6
- absorb: float32 [128, 128, 128], P(('groups', 'slab')), parts along dimension 0, may hold values from 0.5 to 2
- kernel: float32 [16, 8], P('groups'), parts along dimension 0, may hold values from 0.05 to 1
- inv_width: float32 [2], P('groups'), parts along dimension 0, may hold values from 0.5 to 2
Outputs:
- step_dir: float32 [16, 64, 128, 128], P(('groups', 'dom'), 'slab'), parts along dimension 0
The draws below stay inside these ranges and needn't reach their ends.
There are 2 independent parts, one for each index of `groups`. The reference program is written for one: setup_inputs(seed, part) draws one part's arguments, and reference() takes and returns one part's arrays. A program takes and returns all parts, laid end to end along the dimension named above; each array names one. Nothing has to cross between parts.
All inputs are finite; a program needn't handle non-finite values.
Results may differ from the reference program's by a relative error of at most 0.0021.
Values may be sent and summed in bfloat16 or wider, within the bound.
No kernel may reach another device: no remote copies, remote signals or barrier semaphores. Data moves between devices by JAX's collectives and lax.ppermute only.
A program may use at most 64 MiB of HBM per device.

```python
import math
import jax
import jax.numpy as jnp
from jax import lax

NX = 128
NY = 128
NZ = 64
PARTICLES = 8


def block_levels(rng, shape, shards, low, high):
    loudness, own = 1.0, jax.random.fold_in(rng, 6)
    for position, parts in shards:
        steps = jnp.exp(jax.random.uniform(jax.random.fold_in(own, position), (parts,), jnp.float32, low / len(shards), high / len(shards)))
        loudness = loudness * jnp.repeat(steps, shape[position] // parts).reshape([-1 if axis == position else 1 for axis in range(len(shape))])
    return loudness


def normal_values(stream_key, shape, scale, reach, shards=(), dtype=jnp.bfloat16):
    gain = block_levels(stream_key, shape, shards, -0.22, 0.18) if shards else 1.0
    entries = jax.random.normal(stream_key, shape, jnp.float32) * scale * gain
    return jnp.minimum(jnp.maximum(entries, -reach), reach).astype(dtype)


def setup_inputs(seed: int = 0, part: int = 0) -> dict:
    seeds = jax.random.split(jax.random.key(seed), 9)
    own_keys = jax.random.split(jax.random.fold_in(seeds[8], part), 9)
    particles = normal_values(own_keys[0], (PARTICLES, NZ, NX, NY), 0.5, 3.0, ((0, 8), (1, 2)), jnp.float32)
    state_zero = normal_values(own_keys[1], (PARTICLES, NZ, NX, NY), 1.0, 6.0, ((0, 8), (1, 2)))
    state_one = normal_values(own_keys[2], (PARTICLES, NZ, NX, NY), 1.0, 6.0, ((0, 8), (1, 2)))
    source = normal_values(own_keys[3], (NZ, NX, NY), 1.0, 6.0, ((0, 2),), jnp.float32)
    observed = normal_values(own_keys[4], (NZ, NX, NY), 1.0, 6.0, ((0, 2),), jnp.float32)
    absorb = jnp.clip(jnp.exp(math.log(2.0) - 1.3862944 * jax.random.uniform(own_keys[5], (NZ, NX, NY), jnp.float32) ** block_levels(own_keys[5], (NZ, NX, NY), ((0, 2),), -0.2, 0.2)), 0.5, 2.0)
    kernel = jnp.clip(jax.random.uniform(own_keys[6], (PARTICLES, PARTICLES), jnp.float32, 0.05, 1.0), 0.05, 1.0)
    inv_width = jnp.clip(jnp.exp(jax.random.uniform(own_keys[7], (1,), jnp.float32, math.log(0.5), math.log(2.0))), 0.5, 2.0)
    return {"particles": particles, "state_zero": state_zero, "state_one": state_one, "source": source, "observed": observed, "absorb": absorb, "kernel": kernel, "inv_width": inv_width}


misfit_weight = 8.0


def neighbours(values):
    lead = [(0, 0)] * (values.ndim - 3)
    padded = jnp.pad(values, lead + [(1, 1), (1, 1), (1, 1)])
    total = padded[..., 2:, 1:-1, 1:-1] + padded[..., :-2, 1:-1, 1:-1]
    total = total + padded[..., 1:-1, 2:, 1:-1] + padded[..., 1:-1, :-2, 1:-1]
    total = total + padded[..., 1:-1, 1:-1, 2:] + padded[..., 1:-1, 1:-1, :-2]
    return total


def reference(particles, state_zero, state_one, source, observed, absorb, kernel, inv_width):
    repulsion = inv_width[0]

    def particle_term(members):
        log_field, first_state, second_state = members
        near_zero = neighbours(first_state.astype(jnp.float32))
        near_one = neighbours(second_state.astype(jnp.float32))
        conduct = jnp.exp(log_field)
        denominator = 6.0 * conduct + absorb
        state_two = (source + conduct * near_one) / denominator
        adj_two = misfit_weight * (state_two - observed)
        adj_one = neighbours(conduct / denominator * adj_two)
        gradient = -log_field - conduct * (adj_two * (absorb * near_one - 6.0 * source) + adj_one * (absorb * near_zero - 6.0 * source)) / (denominator * denominator)
        return (gradient - repulsion * log_field).astype(jnp.bfloat16)

    carried = lax.map(particle_term, (particles, state_zero, state_one))
    count = particles.shape[0]
    weights = kernel.astype(jnp.bfloat16)
    mixed = jnp.dot(weights.T, carried.reshape(count, -1), preferred_element_type=jnp.float32)
    column_sums = jnp.sum(kernel, axis=0)
    result = mixed.reshape(particles.shape) + repulsion * particles * column_sums[:, None, None, None]
    return result / count
```

```python
import functools

import jax
import jax.numpy as jnp
from jax import lax
from jax.experimental import pallas as pl
from jax.experimental.pallas import tpu as pltpu
from jax.sharding import PartitionSpec as P

misfit_weight = 8.0
f32, bf16 = jnp.float32, jnp.bfloat16
BACK = bf16
HALVES = ("a2a", "pp")
TILE = 32
VMEM = pl.BlockSpec(memory_space=pltpu.VMEM)
ANY = pl.BlockSpec(memory_space=pl.ANY)
SMEM = pl.BlockSpec(memory_space=pltpu.SMEM)
LIMIT = 48 * 1024 * 1024


def params():
    return pltpu.CompilerParams(vmem_limit_bytes=LIMIT)


def band(rows, cols, period):
    r = lax.broadcasted_iota(jnp.int32, (rows, cols), 0)
    c = lax.broadcasted_iota(jnp.int32, (rows, cols), 1)
    gap = (r % period) - (c % period)
    same = (gap == 1) | (gap == -1)
    if rows == cols and rows > period:
        same = same & (r // period == c // period)
    return jnp.where(same, 1.0, 0.0).astype(bf16)


def front_kernel(
    geometry, place, rho, p_h, s0_h, s1_h, src_h, obs_h, ab_h, halo32, halo16, *rest
):
    layers, nx, ny, start, count, parts, split = geometry
    outs, rest = rest[: parts if split else 1], rest[parts if split else 1 :]
    pv, sv, srcv, obsv, abv, w32, whl, g1, g2, nxy, axy, t2, tx, u2, ux, keep, sem = rest
    slab = place[0]
    first = max(start - 1, 0)
    final = min(start + count, layers)
    halo = final == layers
    base = first - 1
    wn = final - first + 1

    def z_of(r):
        return jnp.where(slab == 0, r, layers - 1 - r)

    def copies(r):
        k = r - base
        plain = first <= r <= final
        state0 = plain or (r == start - 1 and r >= 0)
        out = []
        if r < layers:
            z = z_of(r)
            if plain:
                for n, (src, dst) in enumerate(((p_h, pv), (src_h, srcv), (obs_h, obsv), (ab_h, abv))):
                    at = (0, z) if n == 0 else (z,)
                    out.append((src.at[at], dst.at[k], sem.at[n, k]))
            if r >= 0:
                out.append((s1_h.at[0, z], sv.at[k, :, :ny], sem.at[4, k]))
                out.append((s0_h.at[0, z], sv.at[k, :, ny:], sem.at[5, k]))
        else:
            if r == layers:
                for n, dst in enumerate((pv, srcv, obsv, abv)):
                    out.append((halo32.at[n], dst.at[k], sem.at[n, k]))
                out.append((halo16.at[2], sv.at[k, :, ny:], sem.at[5, k]))
            out.append((halo16.at[r - layers], sv.at[k, :, :ny], sem.at[4, k]))
        return [pltpu.make_async_copy(*c) for c in out]

    plan = {r: copies(r) for r in range(base, final + 2)}
    for r in plan:
        for c in plan[r]:
            c.start()
    if base < 0:
        sv[0] = jnp.zeros(sv.shape[1:], sv.dtype)
        w32[0] = jnp.zeros(w32.shape[1:], f32)
    t2[...] = band(2 * ny, 2 * ny, ny)
    u2[...] = band(2 * ny, ny, ny)
    tx[...] = band(nx, nx, nx)
    ux[...] = band(nx, 2 * nx, nx)
    own = 1.0 + rho[0]

    def forward(k):
        states = sv[k]
        nxy[...] = jnp.dot(states, t2[...], preferred_element_type=f32) + jnp.dot(
            tx[...], states, preferred_element_type=f32
        )
        for t in range(0, nx, TILE):
            rows = pl.ds(t, TILE)
            near = nxy[rows, :] + sv[k - 1, rows, :].astype(f32) + sv[k + 1, rows, :].astype(f32)
            near_one, near_zero = near[:, :ny], near[:, ny:]
            p = pv[k, rows, :]
            ab = abv[k, rows, :]
            src = srcv[k, rows, :]
            conduct = jnp.exp(p)
            inverse = 1.0 / (6.0 * conduct + ab)
            ratio = conduct * inverse
            adj_two = misfit_weight * ((src + conduct * near_one) * inverse - obsv[k, rows, :])
            weighted = ratio * adj_two
            w32[k, rows, :] = weighted
            high = weighted.astype(bf16)
            low = (weighted - high.astype(f32)).astype(bf16)
            whl[k % 2, rows, :] = high
            whl[k % 2, pl.ds(nx + t, TILE), :] = low
            scale = ratio * inverse
            six = 6.0 * src
            g1[k % 2, rows, :] = -own * p - scale * (adj_two * (ab * near_one - six))
            g2[k % 2, rows, :] = scale * (ab * near_zero - six)

    def backward(k):
        high, low = whl[k % 2, :nx, :], whl[k % 2, nx:, :]
        wide = jnp.concatenate([high, low], axis=1)
        axy[...] = jnp.dot(wide, u2[...], preferred_element_type=f32) + jnp.dot(
            ux[...], whl[k % 2], preferred_element_type=f32
        )
        for t in range(0, nx, TILE):
            rows = pl.ds(t, TILE)
            adj_one = axy[rows, :] + w32[k - 1, rows, :] + w32[k + 1, rows, :]
            out = (g1[k % 2, rows, :] - adj_one * g2[k % 2, rows, :]).astype(bf16)
            r = k + base - start
            if split:
                keep[pl.ds(pl.multiple_of(r * nx + t, TILE), TILE), :] = out
            else:
                outs[0][r, rows, :] = out

    def wait(rs):
        for r in rs:
            for c in plan[r]:
                c.wait()

    wait(range(base, first + 1))
    for r in range(first, final + 1):
        wait([r + 1])
        forward(r - base)
        if start <= r - 1 < start + count:
            backward(r - 1 - base)
    if split:
        me = place[1]
        size = count * nx // parts
        for s in range(parts):
            at = pl.multiple_of((me ^ s) * size, 16)
            outs[s][...] = keep[pl.ds(at, size), :]


def front(place, rho, arrays, halos, start, count, parts, split):
    _, layers, nx, ny = arrays[0].shape
    first = max(start - 1, 0)
    slots = min(start + count, layers) + 1 - first + 2
    geometry = (layers, nx, ny, start, count, parts, split)
    size = count * nx // parts
    if split:
        shapes = [jax.ShapeDtypeStruct((size, ny), bf16)] * parts
    else:
        shapes = [jax.ShapeDtypeStruct((count, nx, ny), bf16)]
    if halos is None:
        halos = (arrays[0], arrays[1])
    cells = (slots - 2) * nx * ny
    return pl.pallas_call(
        functools.partial(front_kernel, geometry),
        out_shape=shapes,
        in_specs=[SMEM, SMEM] + [ANY] * 8,
        out_specs=[VMEM] * len(shapes),
        scratch_shapes=[
            pltpu.VMEM((slots, nx, ny), f32),
            pltpu.VMEM((slots, nx, 2 * ny), bf16),
            pltpu.VMEM((slots, nx, ny), f32),
            pltpu.VMEM((slots, nx, ny), f32),
            pltpu.VMEM((slots, nx, ny), f32),
            pltpu.VMEM((slots, nx, ny), f32),
            pltpu.VMEM((2, 2 * nx, ny), bf16),
            pltpu.VMEM((2, nx, ny), f32),
            pltpu.VMEM((2, nx, ny), f32),
            pltpu.VMEM((nx, 2 * ny), f32),
            pltpu.VMEM((nx, ny), f32),
            pltpu.VMEM((2 * ny, 2 * ny), bf16),
            pltpu.VMEM((nx, nx), bf16),
            pltpu.VMEM((2 * ny, ny), bf16),
            pltpu.VMEM((nx, 2 * nx), bf16),
            pltpu.VMEM((count * nx if split else 16, ny), bf16),
            pltpu.SemaphoreType.DMA((6, slots)),
        ],
        compiler_params=params(),
        cost_estimate=pl.CostEstimate(flops=100 * cells, bytes_accessed=20 * cells, transcendentals=cells),
        name="front",
    )(place, rho, *arrays, *halos)


def pack_kernel(place, p_h, s0_h, s1_h, src_h, obs_h, ab_h, out32, out16, sem):
    layers = src_h.shape[0]
    face = jnp.where(place[0] == 0, layers - 1, 0)
    inner = jnp.where(place[0] == 0, layers - 2, 1)
    pairs = [
        (p_h.at[0, face], out32.at[0]),
        (src_h.at[face], out32.at[1]),
        (obs_h.at[face], out32.at[2]),
        (ab_h.at[face], out32.at[3]),
        (s1_h.at[0, face], out16.at[0]),
        (s1_h.at[0, inner], out16.at[1]),
        (s0_h.at[0, face], out16.at[2]),
    ]
    moves = [pltpu.make_async_copy(a, b, sem.at[n]) for n, (a, b) in enumerate(pairs)]
    for m in moves:
        m.start()
    for m in moves:
        m.wait()


def pack(place, arrays):
    _, layers, nx, ny = arrays[0].shape
    return pl.pallas_call(
        pack_kernel,
        out_shape=[jax.ShapeDtypeStruct((4, nx, ny), f32), jax.ShapeDtypeStruct((3, nx, ny), bf16)],
        in_specs=[SMEM] + [ANY] * 6,
        out_specs=[VMEM, VMEM],
        scratch_shapes=[pltpu.SemaphoreType.DMA((7,))],
        compiler_params=params(),
        name="pack",
    )(place, *arrays)


def mix_kernel(parts, split, place, weights, *rest):
    ins, rest = rest[: parts if split else 1], rest[parts if split else 1 :]
    outs, wide = rest[: parts if split else 1], rest[-1]
    rounded = weights[...].astype(bf16).astype(f32)
    for j in range(parts):
        for i in range(parts):
            wide[j * parts + i] = jnp.broadcast_to(rounded[j : j + 1, i : i + 1], wide.shape[1:])
    size, ny = ins[0].shape[-2:]
    me = place[1] if split else 0

    def body(step, carry):
        rows = pl.ds(pl.multiple_of(step * TILE, TILE), TILE)
        fields = []
        for s in range(parts):
            v = ins[s][rows, :] if split else ins[0][s, rows, :]
            fields.append(v.astype(f32).reshape(TILE // 8, 8, ny))
        for t in range(parts):
            total = 0.0
            for s in range(parts):
                at = (me ^ s) * parts + (me ^ t) if split else s * parts + t
                total = total + fields[s] * wide[at][None]
            out = total.reshape(TILE, ny)
            if split:
                outs[t][rows, :] = out.astype(outs[t].dtype)
            else:
                outs[0][t, rows, :] = out.astype(outs[0].dtype)
        return carry

    lax.fori_loop(0, size // TILE, body, 0)


def mix(place, weights, fields, split):
    parts = weights.shape[0]
    if split:
        shapes = [jax.ShapeDtypeStruct(f.shape, BACK if s else f32) for s, f in enumerate(fields)]
    else:
        shapes = [jax.ShapeDtypeStruct(fields[0].shape, BACK)]
    cells = parts * fields[0].shape[-2] * fields[0].shape[-1]
    return pl.pallas_call(
        functools.partial(mix_kernel, parts, split),
        out_shape=shapes,
        in_specs=[SMEM, VMEM] + [VMEM] * len(fields),
        out_specs=[VMEM] * len(shapes),
        scratch_shapes=[pltpu.VMEM((parts * parts, 8, fields[0].shape[-1]), f32)],
        compiler_params=params(),
        cost_estimate=pl.CostEstimate(flops=2 * parts * cells, bytes_accessed=4 * cells, transcendentals=0),
        name="mix",
    )(place, weights, *fields)


def last_kernel(geometry, place, rho, weights, p_h, *rest):
    layers, nx, ny, start, count, parts, split, chained = geometry
    if chained:
        rest = rest[1:]
    ins, rest = rest[: parts if split else 1], rest[parts if split else 1 :]
    out_h, pv, ov, sem_in, sem_out = rest

    def z_of(r):
        return jnp.where(place[0] == 0, r, layers - 1 - r)

    loads = [
        pltpu.make_async_copy(p_h.at[0, z_of(start + k)], pv.at[pl.ds(k * nx, nx)], sem_in.at[k])
        for k in range(count)
    ]
    stores = [
        pltpu.make_async_copy(ov.at[pl.ds(k * nx, nx)], out_h.at[0, z_of(start + k)], sem_out.at[k])
        for k in range(count)
    ]
    for c in loads:
        c.start()
    column = lax.broadcasted_iota(jnp.int32, weights.shape, 1) == place[1]
    picked = jnp.where(column, weights[...], 0.0)
    sums = jnp.sum(jnp.sum(picked, axis=1, keepdims=True), axis=0, keepdims=True)
    inverse = 1.0 / parts
    gain = rho[0] * sums * inverse

    def apply(mixed, rows):
        ov[rows, :] = mixed.astype(f32) * inverse + pv[rows, :] * gain

    if split:
        for c in loads:
            c.wait()
        size = count * nx // parts
        for s in range(parts):
            apply(ins[s][...], pl.ds(pl.multiple_of((place[1] ^ s) * size, 16), size))
        for c in stores:
            c.start()
    else:
        for k in range(count):
            loads[k].wait()
            apply(ins[0][k], pl.ds(k * nx, nx))
            stores[k].start()
    for c in stores:
        c.wait()


def last(place, rho, weights, particles, mixed, start, count, split, so_far):
    _, layers, nx, ny = particles.shape
    parts = weights.shape[0]
    chained = so_far is not None
    geometry = (layers, nx, ny, start, count, parts, split, chained)
    extra = [so_far] if chained else []
    cells = count * nx * ny
    return pl.pallas_call(
        functools.partial(last_kernel, geometry),
        out_shape=jax.ShapeDtypeStruct(particles.shape, f32),
        in_specs=[SMEM, SMEM, VMEM, ANY] + [ANY] * len(extra) + [VMEM] * len(mixed),
        out_specs=ANY,
        scratch_shapes=[
            pltpu.VMEM((count * nx, ny), f32),
            pltpu.VMEM((count * nx, ny), f32),
            pltpu.SemaphoreType.DMA((count,)),
            pltpu.SemaphoreType.DMA((count,)),
        ],
        input_output_aliases={4: 0} if chained else {},
        compiler_params=params(),
        cost_estimate=pl.CostEstimate(flops=4 * cells, bytes_accessed=10 * cells, transcendentals=0),
        name="last",
    )(place, rho, weights, particles, *extra, *mixed)


def shards(particles, state_zero, state_one, source, observed, absorb, kernel, inv_width):
    _, layers, nx, ny = particles.shape
    parts = kernel.shape[0]
    slab, me = lax.axis_index("slab"), lax.axis_index("dom")
    place = jnp.stack([slab, me]).astype(jnp.int32)
    arrays = (particles, state_zero, state_one, source, observed, absorb)

    def hop(value, s):
        return lax.ppermute(value, "dom", [(i, i ^ s) for i in range(parts)]) if s else value

    def whole(value):
        return lax.all_to_all(value, "dom", split_axis=0, concat_axis=0, tiled=True)

    order = [s for s in range(parts) if s & (parts // 2)] + [s for s in range(parts) if not s & (parts // 2)]

    def exchange(fields, split):
        if not split:
            return [whole(fields[0])]
        got = {s: hop(fields[s], s) for s in order}
        return [got[s] for s in range(parts)]

    count = layers // len(HALVES)
    faces = pack(place, arrays)
    swap = [(0, 1), (1, 0)]
    halos = [lax.ppermute(f, "slab", swap) for f in faces]
    result = None
    sent, back = [], []
    for n, kind in enumerate(HALVES):
        split = kind == "pp"
        fields = front(
            place, inv_width, arrays, halos if n == len(HALVES) - 1 else None, n * count, count, parts, split
        )
        if not split:
            fields = [fields[0].reshape(parts, -1, ny)]
        sent.append(exchange(fields, split))
    for n, kind in enumerate(HALVES):
        split = kind == "pp"
        back.append(exchange(mix(place, kernel, sent[n], split), split))
    for n, kind in enumerate(HALVES):
        split = kind == "pp"
        mixed = back[n]
        if not split:
            mixed = [mixed[0].reshape(count, nx, ny)]
        result = last(place, inv_width, kernel, particles, mixed, n * count, count, split, result)
    return result


def solution(mesh):
    return jax.shard_map(
        shards,
        mesh=mesh,
        in_specs=(
            P(("groups", "dom"), "slab", None, None),
            P(("groups", "dom"), "slab", None, None),
            P(("groups", "dom"), "slab", None, None),
            P(("groups", "slab"), None, None),
            P(("groups", "slab"), None, None),
            P(("groups", "slab"), None, None),
            P("groups", None),
            P("groups"),
        ),
        out_specs=P(("groups", "dom"), "slab", None, None),
        check_vma=False,
    )
```

```python
import functools
import math

import jax
import jax.numpy as jnp
from jax import lax
from jax.experimental import pallas as pl
from jax.experimental.pallas import tpu as pltpu
from jax.sharding import PartitionSpec as P

misfit_weight = 8.0
f32, bf16 = jnp.float32, jnp.bfloat16
BACK = bf16
TILE = 32
FRONTS = ((4, 2), (4, 3), (2, 0))
GROUPS = (4, 7)
VMEM = pl.BlockSpec(memory_space=pltpu.VMEM)
ANY = pl.BlockSpec(memory_space=pl.ANY)
SMEM = pl.BlockSpec(memory_space=pltpu.SMEM)
LIMIT = 61184 * 1024
FRONT = 48 * 1024 * 1024
SMALL = 16 * 1024 * 1024


def band(rows, cols, period):
    r = lax.broadcasted_iota(jnp.int32, (rows, cols), 0)
    c = lax.broadcasted_iota(jnp.int32, (rows, cols), 1)
    gap = (r % period) - (c % period)
    same = (gap == 1) | (gap == -1)
    if rows == cols and rows > period:
        same = same & (r // period == c // period)
    return jnp.where(same, 1.0, 0.0).astype(bf16)


def pack_kernel(p_h, s0_h, s1_h, src_h, obs_h, ab_h, faces, states, sem):
    layers = src_h.shape[0]
    slab = lax.axis_index("slab")
    face = jnp.where(slab == 0, layers - 1, 0)
    inner = jnp.where(slab == 0, layers - 2, 1)
    pairs = [(p_h.at[0, face], faces.at[0]), (src_h.at[face], faces.at[1]), (obs_h.at[face], faces.at[2])]
    pairs += [(ab_h.at[face], faces.at[3]), (s1_h.at[0, face], states.at[0]), (s1_h.at[0, inner], states.at[1])]
    pairs += [(s0_h.at[0, face], states.at[2])]
    moves = [pltpu.make_async_copy(a, b, sem.at[n]) for n, (a, b) in enumerate(pairs)]
    for m in moves:
        m.start()
    for m in moves:
        m.wait()
    faces[pl.ds(4, 3)] = states[...].astype(f32)


def pack(arrays):
    _, layers, nx, ny = arrays[0].shape
    return pl.pallas_call(
        pack_kernel,
        out_shape=jax.ShapeDtypeStruct((7, nx, ny), f32),
        in_specs=[ANY] * 6,
        out_specs=VMEM,
        scratch_shapes=[pltpu.VMEM((3, nx, ny), bf16), pltpu.SemaphoreType.DMA((7,))],
        compiler_params=pltpu.CompilerParams(vmem_limit_bytes=LIMIT),
        name="pack",
    )(*arrays)


def front_kernel(geometry, rho, p_h, s0_h, s1_h, src_h, obs_h, ab_h, halo, *rest):
    rest = rest[1:] if geometry[-1] else rest
    layers, nx, ny, count, wide, parts, members, region, _ = geometry
    outs, rest = rest[: len(members)], rest[len(members) :]
    pv, sv, srcv, obsv, abv, w32, whl, g1, g2, nxy, axy, t2, tx, u2, ux, keep, hv, sem = rest
    slab, me = lax.axis_index("slab"), lax.axis_index("dom")
    group = me // len(members) ^ region
    start = group * count
    edge = jnp.clip(start - 2, 0, layers - wide)

    def slot(q):
        r = start - 2 + q
        m = r - edge
        inside = jnp.where(slab == 0, m, wide - 1 - m)
        beyond = wide + 2 if q < 2 and count == layers else wide + (0 if q in (1, count + 2) else 1)
        return jnp.where((r >= 0) & (r < layers), inside, beyond)

    waits, tops, at = [], [], 0
    while at < wide:
        n = min(GROUPS[min(len(waits), len(GROUPS) - 1)], wide - at)
        z = jnp.where(slab == 0, edge + at, layers - edge - at - n)
        into = pl.ds(jnp.where(slab == 0, at, wide - at - n), n)
        pairs = (
            (s1_h.at[0, pl.ds(z, n)], sv.at[into, :, pl.ds(0, ny)]),
            (s0_h.at[0, pl.ds(z, n)], sv.at[into, :, pl.ds(ny, ny)]),
            (p_h.at[0, pl.ds(z, n)], pv.at[into]),
            (src_h.at[pl.ds(z, n)], srcv.at[into]),
            (ab_h.at[pl.ds(z, n)], abv.at[into]),
            (obs_h.at[pl.ds(z, n)], obsv.at[into]),
        )
        waits.append([pltpu.make_async_copy(x, y, sem.at[m, len(waits)]) for m, (x, y) in enumerate(pairs)])
        at += n
        tops.append(at)
    beyond = pltpu.make_async_copy(halo, hv, sem.at[0, len(waits)])
    beyond.start()
    for copies in waits:
        for c in copies:
            c.start()
    t2[...] = band(2 * ny, 2 * ny, ny)
    u2[...] = band(2 * ny, ny, ny)
    tx[...] = band(nx, nx, nx)
    ux[...] = band(nx, 2 * nx, nx)
    own = 1.0 + rho[0]
    beyond.wait()
    face = group == layers // count - 1

    def fill(n):
        return jnp.where(face, hv[n], 0.0)

    pv[wide], srcv[wide], obsv[wide], abv[wide] = fill(0), fill(1), fill(2), jnp.where(face, hv[3], 1.0)
    sv[wide, :, :ny] = fill(4).astype(bf16)
    sv[wide + 1, :, :ny] = fill(5).astype(bf16)
    sv[wide, :, ny:] = fill(6).astype(bf16)
    sv[wide + 1, :, ny:] = jnp.zeros((nx, ny), bf16)
    sv[wide + 2] = jnp.zeros((nx, 2 * ny), bf16)
    if count == layers:
        w32[1] = jnp.zeros((nx, ny), f32)

    def near_dots(q):
        states = sv[slot(q)]
        nxy[q % 2] = jnp.dot(states, t2[...], preferred_element_type=f32) + jnp.dot(
            tx[...], states, preferred_element_type=f32
        )

    def forward(q):
        here, under, over = slot(q), slot(q - 1), slot(q + 1)
        b = q % 2
        for t in range(0, nx, TILE):
            rows = pl.ds(t, TILE)
            near = nxy[b, rows, :] + sv[under, rows, :].astype(f32) + sv[over, rows, :].astype(f32)
            near_one, near_zero = near[:, :ny], near[:, ny:]
            p = pv[here, rows, :]
            ab = abv[here, rows, :]
            src = srcv[here, rows, :]
            conduct = jnp.exp(p)
            inverse = 1.0 / (6.0 * conduct + ab)
            ratio = conduct * inverse
            adj_two = misfit_weight * ((src + conduct * near_one) * inverse - obsv[here, rows, :])
            weighted = ratio * adj_two
            if q == 1:
                weighted = jnp.where(group == 0, 0.0, weighted)
            w32[q, rows, :] = weighted
            if not 2 <= q < count + 2:
                continue
            top = weighted.astype(bf16)
            whl[b, rows, :] = top
            whl[b, pl.ds(nx + t, TILE), :] = (weighted - top.astype(f32)).astype(bf16)
            scale = ratio * inverse
            six = 6.0 * src
            g1[b, rows, :] = -own * p - scale * (adj_two * (ab * near_one - six))
            g2[b, rows, :] = scale * (ab * near_zero - six)

    def adjoint_dots(q):
        b = q % 2
        both = jnp.concatenate([whl[b, :nx, :], whl[b, nx:, :]], axis=1)
        axy[b] = jnp.dot(both, u2[...], preferred_element_type=f32) + jnp.dot(
            ux[...], whl[b], preferred_element_type=f32
        )

    def backward(q):
        b = q % 2
        for t in range(0, nx, TILE):
            rows = pl.ds(t, TILE)
            adj_one = axy[b, rows, :] + w32[q - 1, rows, :] + w32[q + 1, rows, :]
            out = (g1[b, rows, :] - adj_one * g2[b, rows, :]).astype(bf16)
            keep[pl.ds((q - 2) * nx + t, TILE), :] = out

    arrived = 0
    for q in range(1, count + 3):
        while arrived < len(waits) and (arrived == 0 or tops[arrived - 1] < min(q + 4, wide)):
            for c in waits[arrived]:
                c.wait()
            arrived += 1
        if q == 1 and count < layers:
            near_dots(q)
        if q + 1 <= count + 2:
            near_dots(q + 1)
        if q > 1 or count < layers:
            forward(q)
        if 2 <= q < count + 2:
            adjoint_dots(q)
        if q >= 3:
            backward(q - 1)
    size = layers * nx // parts
    for n, s in enumerate(members):
        at = pl.multiple_of(((me ^ s) % len(members)) * size, 16)
        outs[n][...] = keep[pl.ds(at, size), :]


def front(rho, arrays, halo, parts, pieces, region, before):
    _, layers, nx, ny = arrays[0].shape
    count = layers // pieces
    wide = min(count + 4, layers)
    width = parts // pieces
    members = tuple(range(region * width, (region + 1) * width))
    extra = [] if before is None else [before]
    geometry = (layers, nx, ny, count, wide, parts, members, region, len(extra))
    size = layers * nx // parts
    slots = wide + 3
    cells = (count + 2) * nx * ny
    return pl.pallas_call(
        functools.partial(front_kernel, geometry),
        out_shape=[jax.ShapeDtypeStruct((size, ny), bf16)] * width,
        in_specs=[SMEM] + [ANY] * (7 + len(extra)),
        out_specs=[VMEM] * width,
        scratch_shapes=[
            pltpu.VMEM((slots, nx, ny), f32),
            pltpu.VMEM((slots, nx, 2 * ny), bf16),
            pltpu.VMEM((slots, nx, ny), f32),
            pltpu.VMEM((slots, nx, ny), f32),
            pltpu.VMEM((slots, nx, ny), f32),
            pltpu.VMEM((count + 4, nx, ny), f32),
            pltpu.VMEM((2, 2 * nx, ny), bf16),
            pltpu.VMEM((2, nx, ny), f32),
            pltpu.VMEM((2, nx, ny), f32),
            pltpu.VMEM((2, nx, 2 * ny), f32),
            pltpu.VMEM((2, nx, ny), f32),
            pltpu.VMEM((2 * ny, 2 * ny), bf16),
            pltpu.VMEM((nx, nx), bf16),
            pltpu.VMEM((2 * ny, ny), bf16),
            pltpu.VMEM((nx, 2 * nx), bf16),
            pltpu.VMEM((count * nx, ny), bf16),
            pltpu.VMEM((7, nx, ny), f32),
            pltpu.SemaphoreType.DMA((6, wide // min(GROUPS) + 2)),
        ],
        compiler_params=pltpu.CompilerParams(vmem_limit_bytes=FRONT),
        cost_estimate=pl.CostEstimate(flops=100 * cells, bytes_accessed=20 * cells, transcendentals=cells),
        name="front",
    )(rho, *arrays, halo, *extra)


def mix_kernel(parts, steps, weights, *rest):
    ins, outs, wide = rest[: len(steps) or 1], rest[len(steps) or 1 : -1], rest[-1]
    rounded = weights[...].astype(bf16).astype(f32)
    for j in range(parts):
        for i in range(parts):
            wide[j * parts + i] = jnp.broadcast_to(rounded[j : j + 1, i : i + 1], wide.shape[1:])
    size, ny = ins[0].shape[-2:]
    me = lax.axis_index("dom") if steps else 0

    def body(step, carry):
        rows = pl.ds(pl.multiple_of(step * TILE, TILE), TILE)
        fields = []
        for n in range(parts):
            v = ins[n][rows, :] if steps else ins[0][n, rows, :]
            fields.append(v.astype(f32).reshape(TILE // 8, 8, ny))
        for m in range(parts):
            total = 0.0
            for n in range(parts):
                at = (me ^ steps[n]) * parts + (me ^ steps[m]) if steps else n * parts + m
                total = total + fields[n] * wide[at][None]
            out = total.reshape(TILE, ny)
            if steps:
                outs[m][rows, :] = out.astype(outs[m].dtype)
            else:
                outs[0][m, rows, :] = out.astype(outs[0].dtype)
        return carry

    lax.fori_loop(0, size // TILE, body, 0)


def mix(weights, fields, steps):
    parts = weights.shape[0]
    if steps:
        shapes = [jax.ShapeDtypeStruct(f.shape, BACK if s else f32) for s, f in zip(steps, fields)]
    else:
        shapes = [jax.ShapeDtypeStruct(fields[0].shape, BACK)]
    cells = parts * fields[0].shape[-2] * fields[0].shape[-1]
    return pl.pallas_call(
        functools.partial(mix_kernel, parts, steps),
        out_shape=shapes,
        in_specs=[VMEM] * (1 + len(fields)),
        out_specs=[VMEM] * len(shapes),
        scratch_shapes=[pltpu.VMEM((parts * parts, 8, fields[0].shape[-1]), f32)],
        compiler_params=pltpu.CompilerParams(vmem_limit_bytes=SMALL),
        cost_estimate=pl.CostEstimate(flops=2 * parts * cells, bytes_accessed=4 * cells, transcendentals=0),
        name="mix",
    )(weights, *fields)


def last_kernel(geometry, rho, weights, p, *rest):
    layers, nx, ny, start, count, parts, steps, chained = geometry
    ins, (out_h, ov, sem) = rest[: len(steps) or 1], rest[-3:]
    slab, me = lax.axis_index("slab"), lax.axis_index("dom")
    size = count * nx // parts
    column = lax.broadcasted_iota(jnp.int32, weights.shape, 1) == me
    picked = jnp.where(column, weights[...], 0.0)
    sums = jnp.sum(jnp.sum(picked, axis=1, keepdims=True), axis=0, keepdims=True)
    inverse = 1.0 / parts
    gain = rho[0] * sums * inverse
    stores = []
    pieces = [(n, (me ^ s) * size) for n, s in enumerate(steps)] or [(0, 0)]
    span = math.gcd(nx, size) if steps else nx
    for n, at in pieces:
        for t in range(0, size if steps else count * nx, span):
            row = at + t
            layer = start + row // nx
            z = jnp.where(slab == 0, layer, layers - 1 - layer)
            inside = pl.ds(pl.multiple_of(row % nx, 16), span)
            here = ins[n][pl.ds(t, span), :] if steps else ins[n][t // nx]
            place = pl.ds(len(stores) * span, span)
            ov[place, :] = here.astype(f32) * inverse + p[0, z, inside, :] * gain
            move = pltpu.make_async_copy(ov.at[place], out_h.at[0, z, inside], sem.at[len(stores)])
            move.start()
            stores.append(move)
    for c in stores:
        c.wait()


def last(rho, weights, particles, mixed, start, count, steps, so_far):
    _, layers, nx, ny = particles.shape
    parts = weights.shape[0]
    chained = so_far is not None
    geometry = (layers, nx, ny, start, count, parts, steps, chained)
    extra = [so_far] if chained else []
    size = count * nx // parts
    rows = size * len(steps) if steps else count * nx
    moves = rows // (math.gcd(nx, size) if steps else nx)
    cells = rows * ny
    return pl.pallas_call(
        functools.partial(last_kernel, geometry),
        out_shape=jax.ShapeDtypeStruct(particles.shape, f32),
        in_specs=[SMEM, VMEM, VMEM] + [VMEM] * len(mixed) + [ANY] * len(extra),
        out_specs=ANY,
        scratch_shapes=[pltpu.VMEM((rows, ny), f32), pltpu.SemaphoreType.DMA((moves,))],
        input_output_aliases={3 + len(mixed): 0} if chained else {},
        compiler_params=pltpu.CompilerParams(vmem_limit_bytes=SMALL),
        cost_estimate=pl.CostEstimate(flops=4 * cells, bytes_accessed=10 * cells, transcendentals=0),
        name="last",
    )(rho, weights, particles, *mixed, *extra)


def shards(particles, state_zero, state_one, source, observed, absorb, kernel, inv_width):
    _, layers, nx, ny = particles.shape
    parts = kernel.shape[0]
    arrays = (particles, state_zero, state_one, source, observed, absorb)
    far, near = tuple(range(parts // 2, parts)), tuple(range(1, parts // 2))
    order = (far[0], *near[:1], *far[1:], *near[1:], 0)

    def hop(value, s):
        return lax.ppermute(value, "dom", [(i, i ^ s) for i in range(parts)])

    def hops(fields):
        return [hop(fields[s], s) if s else fields[0] for s in order]

    halo = lax.ppermute(pack(arrays), "slab", [(0, 1), (1, 0)])
    fields, got = {}, [None]
    for pieces, region in FRONTS:
        width = parts // pieces
        got = front(inv_width, arrays, halo, parts, pieces, region, got[0])
        fields.update(zip(range(region * width, (region + 1) * width), got))
    got = hops(fields)
    got = dict(zip(order, mix(kernel, got, order)))
    got = dict(zip(order, hops(got)))
    return last(inv_width, kernel, particles, [got[s] for s in order], 0, layers, order, None)


def solution(mesh):
    return jax.shard_map(
        shards,
        mesh=mesh,
        in_specs=(
            P(("groups", "dom"), "slab", None, None),
            P(("groups", "dom"), "slab", None, None),
            P(("groups", "dom"), "slab", None, None),
            P(("groups", "slab"), None, None),
            P(("groups", "slab"), None, None),
            P(("groups", "slab"), None, None),
            P("groups", None),
            P("groups"),
        ),
        out_specs=P(("groups", "dom"), "slab", None, None),
        check_vma=False,
    )
```

```python
import functools
import math

import jax
import jax.numpy as jnp
from jax import lax
from jax.experimental import pallas as pl
from jax.experimental.pallas import tpu as pltpu
from jax.sharding import PartitionSpec as P

misfit_weight = 8.0
f32, bf16 = jnp.float32, jnp.bfloat16
BACK = bf16
TILE = 32
INORDER = lambda f, n: (*f[len(f)//2:], *f[:len(f)//2], *n)
HELD = ()
LOAD = 54 * 1024 * 1024
FRONTS = ((4, 2), (2, 0), (4, 3))
GROUPS = (6, 7)
VMEM = pl.BlockSpec(memory_space=pltpu.VMEM)
ANY = pl.BlockSpec(memory_space=pl.ANY)
SMEM = pl.BlockSpec(memory_space=pltpu.SMEM)
LIMIT = 61184 * 1024
FRONT = 48 * 1024 * 1024
SMALL = 16 * 1024 * 1024


def band(rows, cols, period):
    r = lax.broadcasted_iota(jnp.int32, (rows, cols), 0)
    c = lax.broadcasted_iota(jnp.int32, (rows, cols), 1)
    gap = (r % period) - (c % period)
    same = (gap == 1) | (gap == -1)
    if rows == cols and rows > period:
        same = same & (r // period == c // period)
    return jnp.where(same, 1.0, 0.0).astype(bf16)


def pack_kernel(p_h, s0_h, s1_h, src_h, obs_h, ab_h, faces, states, sem):
    layers = src_h.shape[0]
    slab = lax.axis_index("slab")
    face = jnp.where(slab == 0, layers - 1, 0)
    inner = jnp.where(slab == 0, layers - 2, 1)
    pairs = [(p_h.at[0, face], faces.at[0]), (src_h.at[face], faces.at[1]), (obs_h.at[face], faces.at[2])]
    pairs += [(ab_h.at[face], faces.at[3]), (s1_h.at[0, face], states.at[0]), (s1_h.at[0, inner], states.at[1])]
    pairs += [(s0_h.at[0, face], states.at[2])]
    moves = [pltpu.make_async_copy(a, b, sem.at[n]) for n, (a, b) in enumerate(pairs)]
    for m in moves:
        m.start()
    for m in moves:
        m.wait()
    faces[pl.ds(4, 3)] = states[...].astype(f32)


def pack(arrays):
    _, layers, nx, ny = arrays[0].shape
    return pl.pallas_call(
        pack_kernel,
        out_shape=jax.ShapeDtypeStruct((7, nx, ny), f32),
        in_specs=[ANY] * 6,
        out_specs=VMEM,
        scratch_shapes=[pltpu.VMEM((3, nx, ny), bf16), pltpu.SemaphoreType.DMA((7,))],
        compiler_params=pltpu.CompilerParams(vmem_limit_bytes=LIMIT),
        name="pack",
    )(*arrays)


def window(layers, count, group):
    wide = min(count + 4, layers)
    return wide, jnp.clip(group * count - 2, 0, layers - wide)


def load_kernel(layers, count, width, region, *refs):
    sources, held, sem = refs[:3], refs[3:6], refs[6]
    slab, me = lax.axis_index("slab"), lax.axis_index("dom")
    wide, edge = window(layers, count, me // width ^ region)
    z = pl.ds(jnp.where(slab == 0, edge, layers - edge - wide), wide)
    moves = [pltpu.make_async_copy(x.at[z], y, sem.at[n]) for n, (x, y) in enumerate(zip(sources, held))]
    for m in moves:
        m.start()
    for m in moves:
        m.wait()


def load(fields, parts, pieces, region):
    layers, nx, ny = fields[0].shape
    count = layers // pieces
    wide = min(count + 4, layers)
    return pl.pallas_call(
        functools.partial(load_kernel, layers, count, parts // pieces, region),
        out_shape=[jax.ShapeDtypeStruct((wide, nx, ny), f32)] * 3,
        in_specs=[ANY] * 3,
        out_specs=[VMEM] * 3,
        scratch_shapes=[pltpu.SemaphoreType.DMA((3,))],
        compiler_params=pltpu.CompilerParams(vmem_limit_bytes=LOAD),
        cost_estimate=pl.CostEstimate(flops=0, bytes_accessed=24 * wide * nx * ny, transcendentals=0),
        name="load",
    )(*fields)


def front_kernel(geometry, rho, p, s0, s1, src, obs, ab, halo, *rest):
    layers, nx, ny, count, parts, members, region, held, skip = geometry
    outs, rest = rest[skip : skip + len(members)], rest[skip + len(members) :]
    if not held:
        here, sem, rest = rest[:3], rest[3], rest[4:]
    w32, whl, g1, g2, nxy, axy, t2, tx, u2, ux, keep, pe, srce, obse, abe, se = rest
    slab, me = lax.axis_index("slab"), lax.axis_index("dom")
    group = me // len(members) ^ region
    start = group * count
    t2[...] = band(2 * ny, 2 * ny, ny)
    u2[...] = band(2 * ny, ny, ny)
    tx[...] = band(nx, nx, nx)
    ux[...] = band(nx, 2 * nx, nx)
    own = 1.0 + rho[0]
    low, high = group == 0, group == layers // count - 1

    wide, edge = window(layers, count, group)
    waits, tops = [], []
    if not held:
        at = 0
        while at < wide:
            n = min(GROUPS[min(len(waits), len(GROUPS) - 1)], wide - at)
            z = pl.ds(jnp.where(slab == 0, edge + at, layers - edge - at - n), n)
            into = pl.ds(jnp.where(slab == 0, at, wide - at - n), n)
            pairs = zip((src, obs, ab), here)
            waits.append([pltpu.make_async_copy(x.at[z], y.at[into], sem.at[m, len(waits)]) for m, (x, y) in enumerate(pairs)])
            at += n
            tops.append(at)
        for copies in waits:
            for c in copies:
                c.start()
        src, obs, ab = here

    def z_of(q):
        r = jnp.clip(start - 2 + q, 0, layers - 1)
        return jnp.where(slab == 0, r, layers - 1 - r)

    def w_of(q):
        m = jnp.clip(start - 2 + q, 0, layers - 1) - edge
        return jnp.where(slab == 0, m, wide - 1 - m)

    for e, q in enumerate((0, 1, count + 2, count + 3)):
        z = z_of(q)
        outer = low if e < 2 else high
        one = jnp.where(outer, 0.0 if e < 2 else halo[4 if e == 2 else 5], s1[0, z].astype(f32))
        zero = jnp.where(outer, 0.0 if e < 2 else halo[6], s0[0, z].astype(f32))
        se[e, :, :ny] = one.astype(bf16)
        se[e, :, ny:] = zero.astype(bf16)

    def border(q):
        z, w = z_of(q), w_of(q)
        e = 0 if q == 1 else 1
        pe[e] = jnp.where(high, halo[0], p[0, z]) if e else p[0, z]
        srce[e] = jnp.where(high, halo[1], src[w]) if e else src[w]
        obse[e] = jnp.where(high, halo[2], obs[w]) if e else obs[w]
        abe[e] = jnp.where(high, halo[3], ab[w]) if e else ab[w]

    def inside(q):
        return 2 <= q < count + 2

    def states(q, rows):
        if inside(q):
            z = z_of(q)
            return jnp.concatenate([s1[0, z, rows, :], s0[0, z, rows, :]], axis=1)
        return se[q if q < 2 else q - count, rows, :]

    def fields(q, rows):
        if inside(q):
            w = w_of(q)
            return p[0, z_of(q), rows, :], src[w, rows, :], obs[w, rows, :], ab[w, rows, :]
        e = 0 if q == 1 else 1
        return pe[e, rows, :], srce[e, rows, :], obse[e, rows, :], abe[e, rows, :]

    def near_dots(q):
        here = states(q, slice(None))
        nxy[q % 2] = jnp.dot(here, t2[...], preferred_element_type=f32) + jnp.dot(
            tx[...], here, preferred_element_type=f32
        )

    def forward(q):
        b = q % 2
        for t in range(0, nx, TILE):
            rows = pl.ds(t, TILE)
            near = nxy[b, rows, :] + states(q - 1, rows).astype(f32) + states(q + 1, rows).astype(f32)
            near_one, near_zero = near[:, :ny], near[:, ny:]
            log_field, supply, seen, decay = fields(q, rows)
            conduct = jnp.exp(log_field)
            inverse = 1.0 / (6.0 * conduct + decay)
            ratio = conduct * inverse
            adj_two = misfit_weight * ((supply + conduct * near_one) * inverse - seen)
            weighted = ratio * adj_two
            if q == 1:
                weighted = jnp.where(low, 0.0, weighted)
            w32[q, rows, :] = weighted
            if not inside(q):
                continue
            top = weighted.astype(bf16)
            whl[b, rows, :] = top
            whl[b, pl.ds(nx + t, TILE), :] = (weighted - top.astype(f32)).astype(bf16)
            scale = ratio * inverse
            six = 6.0 * supply
            g1[b, rows, :] = -own * log_field - scale * (adj_two * (decay * near_one - six))
            g2[b, rows, :] = scale * (decay * near_zero - six)

    def adjoint_dots(q):
        b = q % 2
        both = jnp.concatenate([whl[b, :nx, :], whl[b, nx:, :]], axis=1)
        axy[b] = jnp.dot(both, u2[...], preferred_element_type=f32) + jnp.dot(
            ux[...], whl[b], preferred_element_type=f32
        )

    def backward(q):
        b = q % 2
        for t in range(0, nx, TILE):
            rows = pl.ds(t, TILE)
            adj_one = axy[b, rows, :] + w32[q - 1, rows, :] + w32[q + 1, rows, :]
            out = (g1[b, rows, :] - adj_one * g2[b, rows, :]).astype(bf16)
            keep[pl.ds((q - 2) * nx + t, TILE), :] = out

    arrived = 0
    near_dots(1)
    for q in range(1, count + 3):
        while arrived < len(waits) and (arrived == 0 or tops[arrived - 1] < min(q + 3, wide)):
            for c in waits[arrived]:
                c.wait()
            arrived += 1
        if not inside(q):
            border(q)
        if q + 1 <= count + 2:
            near_dots(q + 1)
        forward(q)
        if inside(q):
            adjoint_dots(q)
        if q >= 3:
            backward(q - 1)
    size = layers * nx // parts
    for n, s in enumerate(members):
        at = pl.multiple_of(((me ^ s) % len(members)) * size, 16)
        outs[n][...] = keep[pl.ds(at, size), :]


def front(rho, arrays, halo, parts, pieces, region, before):
    _, layers, nx, ny = arrays[0].shape
    deep = arrays[3].shape[0]
    count = layers // pieces
    width = parts // pieces
    members = tuple(range(region * width, (region + 1) * width))
    extra = [] if before is None else [before]
    held = deep < layers
    wide = min(count + 4, layers)
    local = [] if held else [pltpu.VMEM((wide, nx, ny), f32)] * 3 + [pltpu.SemaphoreType.DMA((3, wide // min(GROUPS) + 1))]
    geometry = (layers, nx, ny, count, parts, members, region, held, len(extra))
    size = layers * nx // parts
    cells = (count + 2) * nx * ny
    return pl.pallas_call(
        functools.partial(front_kernel, geometry),
        out_shape=[jax.ShapeDtypeStruct((size, ny), bf16)] * width,
        in_specs=[SMEM] + [VMEM] * 3 + [VMEM if held else ANY] * 3 + [VMEM] + [ANY] * len(extra),
        out_specs=[VMEM] * width,
        scratch_shapes=local
        + [
            pltpu.VMEM((count + 4, nx, ny), f32),
            pltpu.VMEM((2, 2 * nx, ny), bf16),
            pltpu.VMEM((2, nx, ny), f32),
            pltpu.VMEM((2, nx, ny), f32),
            pltpu.VMEM((2, nx, 2 * ny), f32),
            pltpu.VMEM((2, nx, ny), f32),
            pltpu.VMEM((2 * ny, 2 * ny), bf16),
            pltpu.VMEM((nx, nx), bf16),
            pltpu.VMEM((2 * ny, ny), bf16),
            pltpu.VMEM((nx, 2 * nx), bf16),
            pltpu.VMEM((count * nx, ny), bf16),
            pltpu.VMEM((2, nx, ny), f32),
            pltpu.VMEM((2, nx, ny), f32),
            pltpu.VMEM((2, nx, ny), f32),
            pltpu.VMEM((2, nx, ny), f32),
            pltpu.VMEM((4, nx, 2 * ny), bf16),
        ],
        compiler_params=pltpu.CompilerParams(vmem_limit_bytes=FRONT),
        cost_estimate=pl.CostEstimate(flops=100 * cells, bytes_accessed=70 * cells, transcendentals=cells),
        name="front",
    )(rho, *arrays, halo, *extra)


def gate_kernel(*refs):
    refs[-1][...] = jnp.zeros_like(refs[-1])


def gate(fields):
    return pl.pallas_call(
        gate_kernel,
        out_shape=jax.ShapeDtypeStruct((8, 128), f32),
        in_specs=[ANY] * len(fields),
        out_specs=VMEM,
        compiler_params=pltpu.CompilerParams(vmem_limit_bytes=SMALL),
        cost_estimate=pl.CostEstimate(flops=1000, bytes_accessed=2000000, transcendentals=0),
        name="gate",
    )(*fields)


def mix_kernel(parts, steps, members, weights, *rest):
    ins, outs, wide = rest[:parts], rest[parts:-1], rest[-1]
    rounded = weights[...].astype(bf16).astype(f32)
    for j in range(parts):
        for i in range(parts):
            wide[j * parts + i] = jnp.broadcast_to(rounded[j : j + 1, i : i + 1], wide.shape[1:])
    size, ny = ins[0].shape[-2:]
    me = lax.axis_index("dom")

    def body(step, carry):
        rows = pl.ds(pl.multiple_of(step * TILE, TILE), TILE)
        fields = []
        for n in range(parts):
            fields.append(ins[n][rows, :].astype(f32).reshape(TILE // 8, 8, ny))
        for m, target in enumerate(members):
            total = 0.0
            for n, s in enumerate(steps):
                total = total + fields[n] * wide[(me ^ s) * parts + (me ^ target)][None]
            outs[m][rows, :] = total.reshape(TILE, ny).astype(outs[m].dtype)
        return carry

    lax.fori_loop(0, size // TILE, body, 0)


def mix(weights, fields, steps, members):
    parts = weights.shape[0]
    shapes = [jax.ShapeDtypeStruct(fields[0].shape, BACK if s else f32) for s in members]
    cells = parts * fields[0].shape[-2] * fields[0].shape[-1]
    return pl.pallas_call(
        functools.partial(mix_kernel, parts, steps, members),
        out_shape=shapes,
        in_specs=[VMEM] * (1 + len(fields)),
        out_specs=[VMEM] * len(shapes),
        scratch_shapes=[pltpu.VMEM((parts * parts, 8, fields[0].shape[-1]), f32)],
        compiler_params=pltpu.CompilerParams(vmem_limit_bytes=SMALL),
        cost_estimate=pl.CostEstimate(flops=2 * parts * cells, bytes_accessed=4 * cells, transcendentals=0),
        name="mix",
    )(weights, *fields)


def last_kernel(geometry, rho, weights, p, *rest):
    layers, nx, ny, start, count, parts, steps, chained = geometry
    ins, (out_h, ov, sem) = rest[: len(steps) or 1], rest[-3:]
    slab, me = lax.axis_index("slab"), lax.axis_index("dom")
    size = count * nx // parts
    column = lax.broadcasted_iota(jnp.int32, weights.shape, 1) == me
    picked = jnp.where(column, weights[...], 0.0)
    sums = jnp.sum(jnp.sum(picked, axis=1, keepdims=True), axis=0, keepdims=True)
    inverse = 1.0 / parts
    gain = rho[0] * sums * inverse
    stores = []
    pieces = [(n, (me ^ s) * size) for n, s in enumerate(steps)] or [(0, 0)]
    span = math.gcd(nx, size) if steps else nx
    for n, at in pieces:
        for t in range(0, size if steps else count * nx, span):
            row = at + t
            layer = start + row // nx
            z = jnp.where(slab == 0, layer, layers - 1 - layer)
            inside = pl.ds(pl.multiple_of(row % nx, 16), span)
            here = ins[n][pl.ds(t, span), :] if steps else ins[n][t // nx]
            place = pl.ds(len(stores) * span, span)
            ov[place, :] = here.astype(f32) * inverse + p[0, z, inside, :] * gain
            move = pltpu.make_async_copy(ov.at[place], out_h.at[0, z, inside], sem.at[len(stores)])
            move.start()
            stores.append(move)
    for c in stores:
        c.wait()


def last(rho, weights, particles, mixed, start, count, steps, so_far):
    _, layers, nx, ny = particles.shape
    parts = weights.shape[0]
    chained = so_far is not None
    geometry = (layers, nx, ny, start, count, parts, steps, chained)
    extra = [so_far] if chained else []
    size = count * nx // parts
    rows = size * len(steps) if steps else count * nx
    moves = rows // (math.gcd(nx, size) if steps else nx)
    cells = rows * ny
    return pl.pallas_call(
        functools.partial(last_kernel, geometry),
        out_shape=jax.ShapeDtypeStruct(particles.shape, f32),
        in_specs=[SMEM, VMEM, VMEM] + [VMEM] * len(mixed) + [ANY] * len(extra),
        out_specs=ANY,
        scratch_shapes=[pltpu.VMEM((rows, ny), f32), pltpu.SemaphoreType.DMA((moves,))],
        input_output_aliases={3 + len(mixed): 0} if chained else {},
        compiler_params=pltpu.CompilerParams(vmem_limit_bytes=SMALL),
        cost_estimate=pl.CostEstimate(flops=4 * cells, bytes_accessed=10 * cells, transcendentals=0),
        name="last",
    )(rho, weights, particles, *mixed, *extra)


def shards(particles, state_zero, state_one, source, observed, absorb, kernel, inv_width):
    _, layers, nx, ny = particles.shape
    parts = kernel.shape[0]
    arrays = (particles, state_zero, state_one, source, observed, absorb)
    far, near = tuple(range(parts // 2, parts)), tuple(range(1, parts // 2))
    order = (far[0], *near[:1], *far[1:], *near[1:], 0)

    def hop(value, s):
        return lax.ppermute(value, "dom", [(i, i ^ s) for i in range(parts)])

    def hops(fields, order):
        return [hop(fields[s], s) if s else fields[0] for s in order]

    halo = lax.ppermute(pack(arrays), "slab", [(0, 1), (1, 0)])
    fields, got = {}, [None]
    for n, (pieces, region) in enumerate(FRONTS):
        width = parts // pieces
        inputs = arrays[:3] + tuple(load(arrays[3:], parts, pieces, region)) if n in HELD else arrays
        got = front(inv_width, inputs, halo, parts, pieces, region, got[0])
        fields.update(zip(range(region * width, (region + 1) * width), got))
    lead = tuple(INORDER(far, near)) + (0,)
    got = hops(fields, lead)
    got = dict(zip(order, mix(kernel, got, lead, order)))
    got = dict(zip(order, hops(got, order)))
    return last(inv_width, kernel, particles, [got[s] for s in order], 0, layers, order, None)


def solution(mesh):
    return jax.shard_map(
        shards,
        mesh=mesh,
        in_specs=(
            P(("groups", "dom"), "slab", None, None),
            P(("groups", "dom"), "slab", None, None),
            P(("groups", "dom"), "slab", None, None),
            P(("groups", "slab"), None, None),
            P(("groups", "slab"), None, None),
            P(("groups", "slab"), None, None),
            P("groups", None),
            P("groups"),
        ),
        out_specs=P(("groups", "dom"), "slab", None, None),
        check_vma=False,
    )
```

```python
import functools
import math

import jax
import jax.numpy as jnp
from jax import lax
from jax.experimental import pallas as pl
from jax.experimental.pallas import tpu as pltpu
from jax.sharding import PartitionSpec as P

misfit_weight = 8.0
f32, bf16 = jnp.float32, jnp.bfloat16
BACK = bf16
TILE = 32
INORDER = lambda f, n: (*f[len(f)//2:], *f[:len(f)//2], *n)
HELD = ()
LOAD = 54 * 1024 * 1024
FRONTS = ((4, 2), (2, 0), (4, 3))
GROUPS = (6, 7)
VMEM = pl.BlockSpec(memory_space=pltpu.VMEM)
ANY = pl.BlockSpec(memory_space=pl.ANY)
SMEM = pl.BlockSpec(memory_space=pltpu.SMEM)
LIMIT = 61184 * 1024
FRONT = 48 * 1024 * 1024
SMALL = 16 * 1024 * 1024


def band(rows, cols, period):
    r = lax.broadcasted_iota(jnp.int32, (rows, cols), 0)
    c = lax.broadcasted_iota(jnp.int32, (rows, cols), 1)
    gap = (r % period) - (c % period)
    same = (gap == 1) | (gap == -1)
    if rows == cols and rows > period:
        same = same & (r // period == c // period)
    return jnp.where(same, 1.0, 0.0).astype(bf16)


def pack_kernel(p_h, s0_h, s1_h, src_h, obs_h, ab_h, faces, states, sem):
    layers = src_h.shape[0]
    slab = lax.axis_index("slab")
    face = jnp.where(slab == 0, layers - 1, 0)
    inner = jnp.where(slab == 0, layers - 2, 1)
    pairs = [(p_h.at[0, face], faces.at[0]), (src_h.at[face], faces.at[1]), (obs_h.at[face], faces.at[2])]
    pairs += [(ab_h.at[face], faces.at[3]), (s1_h.at[0, face], states.at[0]), (s1_h.at[0, inner], states.at[1])]
    pairs += [(s0_h.at[0, face], states.at[2])]
    moves = [pltpu.make_async_copy(a, b, sem.at[n]) for n, (a, b) in enumerate(pairs)]
    for m in moves:
        m.start()
    for m in moves:
        m.wait()
    faces[pl.ds(4, 3)] = states[...].astype(f32)


def pack(arrays):
    _, layers, nx, ny = arrays[0].shape
    return pl.pallas_call(
        pack_kernel,
        out_shape=jax.ShapeDtypeStruct((7, nx, ny), f32),
        in_specs=[ANY] * 6,
        out_specs=VMEM,
        scratch_shapes=[pltpu.VMEM((3, nx, ny), bf16), pltpu.SemaphoreType.DMA((7,))],
        compiler_params=pltpu.CompilerParams(vmem_limit_bytes=LIMIT),
        name="pack",
    )(*arrays)


def window(layers, count, group):
    wide = min(count + 4, layers)
    return wide, jnp.clip(group * count - 2, 0, layers - wide)


def load_kernel(layers, count, width, region, *refs):
    sources, held, sem = refs[:3], refs[3:6], refs[6]
    slab, me = lax.axis_index("slab"), lax.axis_index("dom")
    wide, edge = window(layers, count, me // width ^ region)
    z = pl.ds(jnp.where(slab == 0, edge, layers - edge - wide), wide)
    moves = [pltpu.make_async_copy(x.at[z], y, sem.at[n]) for n, (x, y) in enumerate(zip(sources, held))]
    for m in moves:
        m.start()
    for m in moves:
        m.wait()


def load(fields, parts, pieces, region):
    layers, nx, ny = fields[0].shape
    count = layers // pieces
    wide = min(count + 4, layers)
    return pl.pallas_call(
        functools.partial(load_kernel, layers, count, parts // pieces, region),
        out_shape=[jax.ShapeDtypeStruct((wide, nx, ny), f32)] * 3,
        in_specs=[ANY] * 3,
        out_specs=[VMEM] * 3,
        scratch_shapes=[pltpu.SemaphoreType.DMA((3,))],
        compiler_params=pltpu.CompilerParams(vmem_limit_bytes=LOAD),
        cost_estimate=pl.CostEstimate(flops=0, bytes_accessed=24 * wide * nx * ny, transcendentals=0),
        name="load",
    )(*fields)


def front_kernel(geometry, rho, p, s0, s1, src, obs, ab, halo, *rest):
    layers, nx, ny, count, parts, members, region, held, skip = geometry
    outs, rest = rest[skip : skip + len(members)], rest[skip + len(members) :]
    if not held:
        here, sem, rest = rest[:3], rest[3], rest[4:]
    w32, whl, g1, g2, nxy, axy, t2, tx, u2, ux, keep, pe, srce, obse, abe, se = rest
    slab, me = lax.axis_index("slab"), lax.axis_index("dom")
    group = me // len(members) ^ region
    start = group * count
    t2[...] = band(2 * ny, 2 * ny, ny)
    u2[...] = band(2 * ny, ny, ny)
    tx[...] = band(nx, nx, nx)
    ux[...] = band(nx, 2 * nx, nx)
    own = 1.0 + rho[0]
    low, high = group == 0, group == layers // count - 1

    wide, edge = window(layers, count, group)
    waits, tops = [], []
    if not held:
        at = 0
        while at < wide:
            n = min(GROUPS[min(len(waits), len(GROUPS) - 1)], wide - at)
            z = pl.ds(jnp.where(slab == 0, edge + at, layers - edge - at - n), n)
            into = pl.ds(jnp.where(slab == 0, at, wide - at - n), n)
            pairs = zip((src, obs, ab), here)
            waits.append([pltpu.make_async_copy(x.at[z], y.at[into], sem.at[m, len(waits)]) for m, (x, y) in enumerate(pairs)])
            at += n
            tops.append(at)
        for copies in waits:
            for c in copies:
                c.start()
        src, obs, ab = here

    def z_of(q):
        r = jnp.clip(start - 2 + q, 0, layers - 1)
        return jnp.where(slab == 0, r, layers - 1 - r)

    def w_of(q):
        m = jnp.clip(start - 2 + q, 0, layers - 1) - edge
        return jnp.where(slab == 0, m, wide - 1 - m)

    for e, q in enumerate((0, 1, count + 2, count + 3)):
        z = z_of(q)
        outer = low if e < 2 else high
        one = jnp.where(outer, 0.0 if e < 2 else halo[4 if e == 2 else 5], s1[0, z].astype(f32))
        zero = jnp.where(outer, 0.0 if e < 2 else halo[6], s0[0, z].astype(f32))
        se[e, :, :ny] = one.astype(bf16)
        se[e, :, ny:] = zero.astype(bf16)

    def border(q):
        z, w = z_of(q), w_of(q)
        e = 0 if q == 1 else 1
        pe[e] = jnp.where(high, halo[0], p[0, z]) if e else p[0, z]
        srce[e] = jnp.where(high, halo[1], src[w]) if e else src[w]
        obse[e] = jnp.where(high, halo[2], obs[w]) if e else obs[w]
        abe[e] = jnp.where(high, halo[3], ab[w]) if e else ab[w]

    def inside(q):
        return 2 <= q < count + 2

    def states(q, rows):
        if inside(q):
            z = z_of(q)
            return jnp.concatenate([s1[0, z, rows, :], s0[0, z, rows, :]], axis=1)
        return se[q if q < 2 else q - count, rows, :]

    def fields(q, rows):
        if inside(q):
            w = w_of(q)
            return p[0, z_of(q), rows, :], src[w, rows, :], obs[w, rows, :], ab[w, rows, :]
        e = 0 if q == 1 else 1
        return pe[e, rows, :], srce[e, rows, :], obse[e, rows, :], abe[e, rows, :]

    def near_dots(q):
        here = states(q, slice(None))
        nxy[q % 2] = jnp.dot(here, t2[...], preferred_element_type=f32) + jnp.dot(
            tx[...], here, preferred_element_type=f32
        )

    def forward(q):
        b = q % 2
        for t in range(0, nx, TILE):
            rows = pl.ds(t, TILE)
            near = nxy[b, rows, :] + states(q - 1, rows).astype(f32) + states(q + 1, rows).astype(f32)
            near_one, near_zero = near[:, :ny], near[:, ny:]
            log_field, supply, seen, decay = fields(q, rows)
            conduct = jnp.exp(log_field)
            inverse = 1.0 / (6.0 * conduct + decay)
            ratio = conduct * inverse
            adj_two = misfit_weight * ((supply + conduct * near_one) * inverse - seen)
            weighted = ratio * adj_two
            if q == 1:
                weighted = jnp.where(low, 0.0, weighted)
            w32[q, rows, :] = weighted
            if not inside(q):
                continue
            top = weighted.astype(bf16)
            whl[b, rows, :] = top
            whl[b, pl.ds(nx + t, TILE), :] = (weighted - top.astype(f32)).astype(bf16)
            scale = ratio * inverse
            six = 6.0 * supply
            g1[b, rows, :] = -own * log_field - scale * (adj_two * (decay * near_one - six))
            g2[b, rows, :] = scale * (decay * near_zero - six)

    def adjoint_dots(q):
        b = q % 2
        both = jnp.concatenate([whl[b, :nx, :], whl[b, nx:, :]], axis=1)
        axy[b] = jnp.dot(both, u2[...], preferred_element_type=f32) + jnp.dot(
            ux[...], whl[b], preferred_element_type=f32
        )

    def backward(q):
        b = q % 2
        for t in range(0, nx, TILE):
            rows = pl.ds(t, TILE)
            adj_one = axy[b, rows, :] + w32[q - 1, rows, :] + w32[q + 1, rows, :]
            out = (g1[b, rows, :] - adj_one * g2[b, rows, :]).astype(bf16)
            keep[pl.ds((q - 2) * nx + t, TILE), :] = out

    arrived = 0
    near_dots(1)
    for q in range(1, count + 3):
        while arrived < len(waits) and (arrived == 0 or tops[arrived - 1] < min(q + 3, wide)):
            for c in waits[arrived]:
                c.wait()
            arrived += 1
        if not inside(q):
            border(q)
        if q + 1 <= count + 2:
            near_dots(q + 1)
        forward(q)
        if inside(q):
            adjoint_dots(q)
        if q >= 3:
            backward(q - 1)
    size = layers * nx // parts
    for n, s in enumerate(members):
        at = pl.multiple_of(((me ^ s) % len(members)) * size, 16)
        outs[n][...] = keep[pl.ds(at, size), :]


def front(rho, arrays, halo, parts, pieces, region, before):
    _, layers, nx, ny = arrays[0].shape
    deep = arrays[3].shape[0]
    count = layers // pieces
    width = parts // pieces
    members = tuple(range(region * width, (region + 1) * width))
    extra = [] if before is None else [before]
    held = deep < layers
    wide = min(count + 4, layers)
    local = [] if held else [pltpu.VMEM((wide, nx, ny), f32)] * 3 + [pltpu.SemaphoreType.DMA((3, wide // min(GROUPS) + 1))]
    geometry = (layers, nx, ny, count, parts, members, region, held, len(extra))
    size = layers * nx // parts
    cells = (count + 2) * nx * ny
    return pl.pallas_call(
        functools.partial(front_kernel, geometry),
        out_shape=[jax.ShapeDtypeStruct((size, ny), bf16)] * width,
        in_specs=[SMEM] + [VMEM] * 3 + [VMEM if held else ANY] * 3 + [VMEM] + [ANY] * len(extra),
        out_specs=[VMEM] * width,
        scratch_shapes=local
        + [
            pltpu.VMEM((count + 4, nx, ny), f32),
            pltpu.VMEM((2, 2 * nx, ny), bf16),
            pltpu.VMEM((2, nx, ny), f32),
            pltpu.VMEM((2, nx, ny), f32),
            pltpu.VMEM((2, nx, 2 * ny), f32),
            pltpu.VMEM((2, nx, ny), f32),
            pltpu.VMEM((2 * ny, 2 * ny), bf16),
            pltpu.VMEM((nx, nx), bf16),
            pltpu.VMEM((2 * ny, ny), bf16),
            pltpu.VMEM((nx, 2 * nx), bf16),
            pltpu.VMEM((count * nx, ny), bf16),
            pltpu.VMEM((2, nx, ny), f32),
            pltpu.VMEM((2, nx, ny), f32),
            pltpu.VMEM((2, nx, ny), f32),
            pltpu.VMEM((2, nx, ny), f32),
            pltpu.VMEM((4, nx, 2 * ny), bf16),
        ],
        compiler_params=pltpu.CompilerParams(vmem_limit_bytes=FRONT),
        cost_estimate=pl.CostEstimate(flops=100 * cells, bytes_accessed=70 * cells, transcendentals=cells),
        name="front",
    )(rho, *arrays, halo, *extra)


def gate_kernel(*refs):
    refs[-1][...] = jnp.zeros_like(refs[-1])


def gate(fields):
    return pl.pallas_call(
        gate_kernel,
        out_shape=jax.ShapeDtypeStruct((8, 128), f32),
        in_specs=[ANY] * len(fields),
        out_specs=VMEM,
        compiler_params=pltpu.CompilerParams(vmem_limit_bytes=SMALL),
        cost_estimate=pl.CostEstimate(flops=1000, bytes_accessed=2000000, transcendentals=0),
        name="gate",
    )(*fields)


def mix_kernel(parts, steps, members, weights, *rest):
    ins, outs, wide = rest[:parts], rest[parts:-1], rest[-1]
    rounded = weights[...].astype(bf16).astype(f32)
    for j in range(parts):
        for i in range(parts):
            wide[j * parts + i] = jnp.broadcast_to(rounded[j : j + 1, i : i + 1], wide.shape[1:])
    size, ny = ins[0].shape[-2:]
    me = lax.axis_index("dom")

    def body(step, carry):
        rows = pl.ds(pl.multiple_of(step * TILE, TILE), TILE)
        fields = []
        for n in range(parts):
            fields.append(ins[n][rows, :].astype(f32).reshape(TILE // 8, 8, ny))
        for m, target in enumerate(members):
            total = 0.0
            for n, s in enumerate(steps):
                total = total + fields[n] * wide[(me ^ s) * parts + (me ^ target)][None]
            outs[m][rows, :] = total.reshape(TILE, ny).astype(outs[m].dtype)
        return carry

    lax.fori_loop(0, size // TILE, body, 0)


def mix(weights, fields, steps, members):
    parts = weights.shape[0]
    shapes = [jax.ShapeDtypeStruct(fields[0].shape, BACK if s else f32) for s in members]
    cells = parts * fields[0].shape[-2] * fields[0].shape[-1]
    return pl.pallas_call(
        functools.partial(mix_kernel, parts, steps, members),
        out_shape=shapes,
        in_specs=[VMEM] * (1 + len(fields)),
        out_specs=[VMEM] * len(shapes),
        scratch_shapes=[pltpu.VMEM((parts * parts, 8, fields[0].shape[-1]), f32)],
        compiler_params=pltpu.CompilerParams(vmem_limit_bytes=SMALL),
        cost_estimate=pl.CostEstimate(flops=2 * parts * cells, bytes_accessed=4 * cells, transcendentals=0),
        name="mix",
    )(weights, *fields)


def last_kernel(geometry, rho, weights, p, *rest):
    layers, nx, ny, start, count, parts, steps, chained = geometry
    ins, (out_h, ov, sem) = rest[: len(steps) or 1], rest[-3:]
    slab, me = lax.axis_index("slab"), lax.axis_index("dom")
    size = count * nx // parts
    column = lax.broadcasted_iota(jnp.int32, weights.shape, 1) == me
    picked = jnp.where(column, weights[...], 0.0)
    sums = jnp.sum(jnp.sum(picked, axis=1, keepdims=True), axis=0, keepdims=True)
    inverse = 1.0 / parts
    gain = rho[0] * sums * inverse
    stores = []
    pieces = [(n, (me ^ s) * size) for n, s in enumerate(steps)] or [(0, 0)]
    span = math.gcd(nx, size) if steps else nx
    for n, at in pieces:
        for t in range(0, size if steps else count * nx, span):
            row = at + t
            layer = start + row // nx
            z = jnp.where(slab == 0, layer, layers - 1 - layer)
            inside = pl.ds(pl.multiple_of(row % nx, 16), span)
            here = ins[n][pl.ds(t, span), :] if steps else ins[n][t // nx]
            place = pl.ds(len(stores) * span, span)
            ov[place, :] = here.astype(f32) * inverse + p[0, z, inside, :] * gain
            move = pltpu.make_async_copy(ov.at[place], out_h.at[0, z, inside], sem.at[len(stores)])
            move.start()
            stores.append(move)
    for c in stores:
        c.wait()


def last(rho, weights, particles, mixed, start, count, steps, so_far):
    _, layers, nx, ny = particles.shape
    parts = weights.shape[0]
    chained = so_far is not None
    geometry = (layers, nx, ny, start, count, parts, steps, chained)
    extra = [so_far] if chained else []
    size = count * nx // parts
    rows = size * len(steps) if steps else count * nx
    moves = rows // (math.gcd(nx, size) if steps else nx)
    cells = rows * ny
    return pl.pallas_call(
        functools.partial(last_kernel, geometry),
        out_shape=jax.ShapeDtypeStruct(particles.shape, f32),
        in_specs=[SMEM, VMEM, VMEM] + [VMEM] * len(mixed) + [ANY] * len(extra),
        out_specs=ANY,
        scratch_shapes=[pltpu.VMEM((rows, ny), f32), pltpu.SemaphoreType.DMA((moves,))],
        input_output_aliases={3 + len(mixed): 0} if chained else {},
        compiler_params=pltpu.CompilerParams(vmem_limit_bytes=SMALL),
        cost_estimate=pl.CostEstimate(flops=4 * cells, bytes_accessed=10 * cells, transcendentals=0),
        name="last",
    )(rho, weights, particles, *mixed, *extra)


def shards(particles, state_zero, state_one, source, observed, absorb, kernel, inv_width):
    _, layers, nx, ny = particles.shape
    parts = kernel.shape[0]
    arrays = (particles, state_zero, state_one, source, observed, absorb)
    far, near = tuple(range(parts // 2, parts)), tuple(range(1, parts // 2))
    order = (far[0], *near[:2], *far[1:], *near[2:], 0)

    def hop(value, s):
        return lax.ppermute(value, "dom", [(i, i ^ s) for i in range(parts)])

    def hops(fields, order):
        return [hop(fields[s], s) if s else fields[0] for s in order]

    halo = lax.ppermute(pack(arrays), "slab", [(0, 1), (1, 0)])
    fields, got = {}, [None]
    for n, (pieces, region) in enumerate(FRONTS):
        width = parts // pieces
        inputs = arrays[:3] + tuple(load(arrays[3:], parts, pieces, region)) if n in HELD else arrays
        got = front(inv_width, inputs, halo, parts, pieces, region, got[0])
        fields.update(zip(range(region * width, (region + 1) * width), got))
    lead = tuple(INORDER(far, near)) + (0,)
    got = hops(fields, lead)
    got = dict(zip(order, mix(kernel, got, lead, order)))
    got = dict(zip(order, hops(got, order)))
    result = None
    for steps in ((*order[:3], 0), order[3:-1]):
        result = last(inv_width, kernel, particles, [got[s] for s in steps], 0, layers, steps, result)
    return result


def solution(mesh):
    return jax.shard_map(
        shards,
        mesh=mesh,
        in_specs=(
            P(("groups", "dom"), "slab", None, None),
            P(("groups", "dom"), "slab", None, None),
            P(("groups", "dom"), "slab", None, None),
            P(("groups", "slab"), None, None),
            P(("groups", "slab"), None, None),
            P(("groups", "slab"), None, None),
            P("groups", None),
            P("groups"),
        ),
        out_specs=P(("groups", "dom"), "slab", None, None),
        check_vma=False,
    )
```
